512 devices in a mesh: pipe: 32 (over z, x_hi), dp: 4 (over y), mp: 4 (over x_lo, core).
Axes of the slice: x: 4 (x_hi: 2, x_lo: 2; x = x_hi * 2 + x_lo), y: 4, z: 16, core: 2. Of those that a mesh axis runs over, the one named last changes fastest.
Arguments:
- act_in: bfloat16 [32, 512, 12288], P('pipe', 'dp', 'mp'), may hold values from -30 to 30
- grad_in: bfloat16 [32, 512, 12288], P('pipe', 'dp', 'mp'), may hold values from -0.8 to 0.8
- stash_far: bfloat16 [32, 512, 12288], P('pipe', 'dp', 'mp'), may hold values from -40 to 40
- up_proj: bfloat16 [32, 12288, 192], P('pipe', 'mp', 'dp'), may hold values from -1 to 1
- down_proj: bfloat16 [32, 192, 12288], P('pipe', 'dp', 'mp'), may hold values from -2 to 2
Outputs:
- act_next: bfloat16 [32, 512, 12288], P('pipe', 'dp', 'mp')
- grad_prev: bfloat16 [32, 512, 12288], P('pipe', 'dp', 'mp')
- up_grad: bfloat16 [32, 12288, 192], P('pipe', 'mp', 'dp')
- down_grad: bfloat16 [32, 192, 12288], P('pipe', 'dp', 'mp')
The draws below stay inside these ranges and needn't reach their ends.
All inputs are finite; a program needn't handle non-finite values.
Results may differ from the reference program's by a relative error of at most 0.03.
Values may be sent and summed in bfloat16 or wider, within the bound.
No kernel may reach another device: no remote copies, remote signals or barrier semaphores. Data moves between devices by JAX's collectives and lax.ppermute only.
A program may use at most 64 MiB of HBM per device.

```python
import jax
import jax.numpy as jnp
from jax import lax

D = 12288
R = 192
ROWS_DEV = 128
SECTIONS = 32
ROWS = 512
N_DP = 4


up_lift = 9.0


down_lift = 60.0


grad_tilt = 0.05


def signed_unit(key, array_shape, lower_end, upper_end):
    subkeys = jax.random.split(key, 2)
    sign_values = (jax.random.randint(subkeys[0], array_shape, 0, 2) * 2 - 1).astype(jnp.float32)
    return sign_values * jax.random.uniform(subkeys[1], array_shape, jnp.float32, lower_end, upper_end)


def shared_parts(key):
    subkeys = jax.random.split(key, 3)
    feature_dir = signed_unit(subkeys[0], (D,), 0.7, 1.3)
    grad_dir = signed_unit(subkeys[1], (D,), 0.7, 1.3)
    rank_signs = (jax.random.randint(subkeys[2], (SECTIONS, R), 0, 2) * 2 - 1).astype(jnp.float32)
    return (feature_dir, grad_dir, rank_signs)


def spread_factors(key):
    subkeys = jax.random.split(key, 4)
    position = jnp.arange(D, dtype=jnp.float32) / (D - 1)
    column = jnp.exp(jnp.log(3.0) * (position - 0.5)) * jax.random.uniform(subkeys[1], (D,), jnp.float32, 0.7, 1.4)
    row_factor = jnp.exp(jax.random.uniform(subkeys[2], (SECTIONS, ROWS, 1), jnp.float32, jnp.log(0.3), jnp.log(3.0)))
    return (subkeys, row_factor, column)


def draw_act_in(key, part):
    key = jax.random.fold_in(key, 11)
    subkeys, row_factor, column = spread_factors(key)
    values = jax.random.truncated_normal(subkeys[0], -4.0, 4.0, (SECTIONS, ROWS, D), jnp.float32)
    return (values * (row_factor * column)).astype(jnp.bfloat16)


def draw_stash_far(key, part):
    feature_dir, grad_dir, rank_signs = shared_parts(key)
    key = jax.random.fold_in(key, 23)
    subkeys, row_factor, column = spread_factors(key)
    values = jax.random.truncated_normal(subkeys[0], -4.0, 4.0, (SECTIONS, ROWS, D), jnp.float32)
    row_pull = signed_unit(jax.random.fold_in(key, 41), (SECTIONS, ROWS, 1), 1.5, 2.5)
    return ((values * column + row_pull * feature_dir) * row_factor).astype(jnp.bfloat16)


def draw_grad_in(key, part):
    feature_dir, grad_dir, rank_signs = shared_parts(key)
    key = jax.random.fold_in(key, 43)
    subkeys = jax.random.split(key, 2)
    noise_part = 0.1 * jax.random.truncated_normal(subkeys[0], -6.0, 6.0, (SECTIONS, ROWS, D), jnp.float32)
    row_pull = signed_unit(subkeys[1], (SECTIONS, ROWS, 1), 1.0, 2.0)
    return (noise_part + grad_tilt * row_pull * grad_dir).astype(jnp.bfloat16)


def draw_up_proj(key, part):
    feature_dir, grad_dir, rank_signs = shared_parts(key)
    key = jax.random.fold_in(key, 31)
    noise_part = jax.random.truncated_normal(key, -5.0, 5.0, (SECTIONS, D, R), jnp.float32) * D ** (-0.5)
    values = noise_part + up_lift / D * feature_dir[None, :, None] * rank_signs[:, None, :]
    return values.astype(jnp.bfloat16)


def draw_down_proj(key, part):
    feature_dir, grad_dir, rank_signs = shared_parts(key)
    key = jax.random.fold_in(key, 37)
    noise_part = jax.random.truncated_normal(key, -5.0, 5.0, (SECTIONS, R, D), jnp.float32) * R ** (-0.5)
    values = noise_part + down_lift / D * rank_signs[:, :, None] * grad_dir[None, None, :]
    return values.astype(jnp.bfloat16)


def setup_inputs(seed: int = 0) -> dict:
    splits = jax.random.split(jax.random.key(seed), 6)
    act_in = draw_act_in(jax.random.fold_in(splits[5], 71), 0)
    grad_in = draw_grad_in(jax.random.fold_in(splits[5], 71), 0)
    stash_far = draw_stash_far(jax.random.fold_in(splits[5], 71), 0)
    up_proj = draw_up_proj(jax.random.fold_in(splits[5], 71), 0)
    down_proj = draw_down_proj(jax.random.fold_in(splits[5], 71), 0)
    return dict(act_in=act_in, grad_in=grad_in, stash_far=stash_far, up_proj=up_proj, down_proj=down_proj)


epsilon = 1e-05

def block_terms(inputs, weight_up):
    squares = lax.optimization_barrier(jnp.sum(jnp.square(inputs.astype(jnp.float32)), axis=-1))
    projected = jnp.dot(inputs, weight_up, preferred_element_type=jnp.float32)
    row_scale = lax.rsqrt(squares / D + epsilon)
    return (projected, row_scale, projected * row_scale[:, None])

def gated(hidden):
    sigmoid_value = jax.nn.sigmoid(hidden)
    return (hidden * sigmoid_value, sigmoid_value * (1.0 + hidden * (1.0 - sigmoid_value)))

def block_sum(left, right):
    left_blocks = left.reshape(N_DP, ROWS_DEV, left.shape[1]).astype(jnp.float32)
    right_blocks = right.reshape(N_DP, ROWS_DEV, right.shape[1]).astype(jnp.float32)
    terms = jnp.einsum('nrd,nrk->ndk', left_blocks, right_blocks).astype(jnp.bfloat16)
    terms = lax.optimization_barrier(terms)
    return lax.optimization_barrier(jnp.sum(terms.astype(jnp.float32), axis=0)).astype(jnp.bfloat16)

def one_section(packed):
    forward_in, cotangent, returned, weight_up, weight_down = packed
    hidden = block_terms(forward_in, weight_up)[2]
    activated = gated(hidden)[0].astype(jnp.bfloat16)
    output = (forward_in.astype(jnp.float32) + jnp.dot(activated, weight_down, preferred_element_type=jnp.float32)).astype(jnp.bfloat16)
    back_proj, back_scale, back_hidden = block_terms(returned, weight_up)
    back_value, back_slope = gated(back_hidden)
    back_act = back_value.astype(jnp.bfloat16)
    grad_act = jnp.dot(cotangent, weight_down.T, preferred_element_type=jnp.float32)
    grad_hidden = grad_act * back_slope
    grad_proj = (grad_hidden * back_scale[:, None]).astype(jnp.bfloat16)
    grad_scale = lax.optimization_barrier(jnp.sum(grad_hidden * back_proj, axis=-1))
    grad_input = cotangent.astype(jnp.float32) + jnp.dot(grad_proj, weight_up.T, preferred_element_type=jnp.float32)
    grad_input = grad_input + returned.astype(jnp.float32) * (-back_scale ** 3 * grad_scale / D)[:, None]
    return (output, grad_input.astype(jnp.bfloat16), block_sum(returned, grad_proj), block_sum(back_act, cotangent))

def reference(act_in, grad_in, stash_far, up_proj, down_proj):
    outputs, grads, up_grad, down_grad = lax.map(one_section, (act_in, grad_in, stash_far[::-1], up_proj, down_proj))
    act_next = jnp.concatenate([jnp.zeros_like(outputs[:1]), outputs[:-1]], axis=0)
    grad_prev = jnp.concatenate([grads[1:], jnp.zeros_like(grads[:1])], axis=0)
    return (act_next, grad_prev, up_grad, down_grad)
```

```python
import jax
import jax.numpy as jnp
from jax import lax
from jax.sharding import PartitionSpec as P

D = 12288


epsilon = 1e-05


def shifted(block, axis, distance):
    devices = range(lax.axis_size(axis))
    route = [(i - distance, i) for i in devices if i - distance in devices]
    return lax.ppermute(block, axis, route)


def mirrored(block, axis):
    last = lax.axis_size(axis) - 1
    return lax.ppermute(block, axis, [(i, last - i) for i in range(last + 1)])


def spread(block, axis):
    copies = jnp.broadcast_to(block[None], (lax.axis_size(axis),) + block.shape)
    return lax.all_to_all(copies, axis, split_axis=0, concat_axis=0, tiled=True)


def summed(block, axis):
    return jnp.sum(spread(block, axis).astype(jnp.float32), axis=0)


def dot(left, right, left_dim, right_dim):
    return lax.dot_general(
        left, right, (((left_dim,), (right_dim,)), ((), ())), preferred_element_type=jnp.float32
    )


def gated(hidden):
    sigmoid_value = jax.nn.sigmoid(hidden)
    return (hidden * sigmoid_value, sigmoid_value * (1.0 + hidden * (1.0 - sigmoid_value)))


def square_rows(inputs):
    squares = jnp.sum(jnp.square(inputs.astype(jnp.float32)), axis=1)
    return jnp.broadcast_to(squares[None], (16, inputs.shape[0]))


def shards(act_in, grad_in, stash_far, up_proj, down_proj):
    forward_in = act_in[0]
    cotangent = grad_in[0]
    group = lax.axis_size("dp")
    rows, features = forward_in.shape
    returned = mirrored(stash_far[0], "pipe")
    up_full = spread(up_proj[0].T, "dp").reshape(-1, features)
    down_full = spread(down_proj[0], "dp").reshape(-1, features)
    rank = up_full.shape[0]
    cotangent_all = spread(cotangent, "dp")

    first = jnp.concatenate(
        [dot(up_full, forward_in, 1, 1), dot(down_full, cotangent, 1, 1), square_rows(forward_in)]
    )
    first = summed(first.astype(jnp.bfloat16), "mp")
    fwd_proj, grad_act, fwd_squares = first[:rank], first[rank : 2 * rank], first[2 * rank]
    fwd_scale = lax.rsqrt(fwd_squares / D + epsilon)
    activated = gated(fwd_proj * fwd_scale[None])[0].astype(jnp.bfloat16)
    output = forward_in.astype(jnp.float32) + dot(activated, down_full, 0, 0)
    act_next = shifted(output.astype(jnp.bfloat16), "pipe", 1)

    second = jnp.concatenate([dot(up_full, returned, 1, 1), square_rows(returned)])
    second = summed(second.astype(jnp.bfloat16), "mp")
    back_proj, back_squares = second[:rank], second[rank]
    back_scale = lax.rsqrt(back_squares / D + epsilon)
    back_value, back_slope = gated(back_proj * back_scale[None])
    back_act = back_value.astype(jnp.bfloat16)
    grad_hidden = grad_act * back_slope
    grad_proj = (grad_hidden * back_scale[None]).astype(jnp.bfloat16)
    grad_scale = jnp.sum(grad_hidden * back_proj, axis=0)
    pull = -(back_scale**3) * grad_scale / D
    grad_input = cotangent.astype(jnp.float32) + dot(grad_proj, up_full, 0, 0)
    grad_input = grad_input + returned.astype(jnp.float32) * pull[:, None]
    grad_prev = shifted(grad_input.astype(jnp.bfloat16), "pipe", -1)

    up_term = dot(grad_proj, returned, 1, 0).astype(jnp.bfloat16)
    up_terms = lax.all_to_all(
        up_term.reshape(group, -1, features), "dp", split_axis=0, concat_axis=0, tiled=True
    )
    up_grad = jnp.sum(up_terms.astype(jnp.float32), axis=0).astype(jnp.bfloat16)
    own_act = lax.all_to_all(
        back_act.reshape(group, -1, rows), "dp", split_axis=0, concat_axis=0, tiled=True
    )
    down_grad = lax.dot_general(
        own_act, cotangent_all, (((0, 2), (0, 1)), ((), ())), preferred_element_type=jnp.float32
    ).astype(jnp.bfloat16)
    return (act_next[None], grad_prev[None], up_grad.T[None], down_grad[None])


def solution(mesh):
    in_specs = (
        P("pipe", "dp", "mp"),
        P("pipe", "dp", "mp"),
        P("pipe", "dp", "mp"),
        P("pipe", "mp", "dp"),
        P("pipe", "dp", "mp"),
    )
    out_specs = (
        P("pipe", "dp", "mp"),
        P("pipe", "dp", "mp"),
        P("pipe", "mp", "dp"),
        P("pipe", "dp", "mp"),
    )
    return jax.shard_map(shards, mesh=mesh, in_specs=in_specs, out_specs=out_specs, check_vma=False)
```

```python
import jax
import jax.numpy as jnp
from jax import lax
from jax.sharding import PartitionSpec as P

D = 12288


epsilon = 1e-05


def shifted(block, axis, distance):
    devices = range(lax.axis_size(axis))
    route = [(i - distance, i) for i in devices if i - distance in devices]
    return lax.ppermute(block, axis, route)


def near_sections(count):
    planes = count // 2
    return [i for i in range(count) if min((2 * (i // 2) + 1) % planes, -(2 * (i // 2) + 1) % planes) <= 3]


def spread(block, axis):
    copies = jnp.broadcast_to(block[None], (lax.axis_size(axis),) + block.shape)
    return lax.all_to_all(copies, axis, split_axis=0, concat_axis=0, tiled=True)


def summed(block, axis):
    return jnp.sum(spread(block, axis).astype(jnp.float32), axis=0)


def from_next(block, axis, distance):
    size = lax.axis_size(axis)
    return lax.ppermute(block, axis, [((i + distance) % size, i) for i in range(size)])


def ring(block, axis):
    return [block] + [from_next(block, axis, k) for k in range(1, lax.axis_size(axis))]


def dot(left, right, left_dim, right_dim):
    return lax.dot_general(
        left, right, (((left_dim,), (right_dim,)), ((), ())), preferred_element_type=jnp.float32
    )


def gated(hidden):
    sigmoid_value = jax.nn.sigmoid(hidden)
    return (hidden * sigmoid_value, sigmoid_value * (1.0 + hidden * (1.0 - sigmoid_value)))


def square_rows(inputs):
    squares = jnp.sum(jnp.square(inputs.astype(jnp.float32)), axis=1)
    return jnp.broadcast_to(squares[None], (16, inputs.shape[0]))


def staged(axis, step, *args):
    shapes = jax.eval_shape(step, *args)
    empty = lambda *_: jax.tree.map(lambda leaf: jnp.zeros(leaf.shape, leaf.dtype), shapes)
    return lax.cond(lax.axis_index(axis) < lax.axis_size(axis), step, empty, *args)


def forward(forward_in, cotangent, up_full, down_full):
    rank = up_full.shape[0]
    first = jnp.concatenate(
        [dot(up_full, forward_in, 1, 1), dot(down_full, cotangent, 1, 1), square_rows(forward_in)]
    )
    first = sum(part.astype(jnp.float32) for part in ring(first.astype(jnp.bfloat16), "mp"))
    fwd_proj, grad_act, fwd_squares = first[:rank], first[rank : 2 * rank], first[2 * rank]
    fwd_scale = lax.rsqrt(fwd_squares / D + epsilon)
    activated = gated(fwd_proj * fwd_scale[None])[0].astype(jnp.bfloat16)
    output = forward_in.astype(jnp.float32) + dot(activated, down_full, 0, 0)
    output = output.astype(jnp.bfloat16)
    middle = lax.axis_size("pipe") // 2
    act_next = lax.ppermute(output, "pipe", [(i - 1, i) for i in range(1, 2 * middle) if i != middle])
    return act_next, output, grad_act


def forward(forward_in, cotangent, up_full, down_full):
    rank = up_full.shape[0]
    first = jnp.concatenate(
        [dot(up_full, forward_in, 1, 1), dot(down_full, cotangent, 1, 1), square_rows(forward_in)]
    )
    first = sum(part.astype(jnp.float32) for part in ring(first.astype(jnp.bfloat16), "mp"))
    fwd_proj, grad_act, fwd_squares = first[:rank], first[rank : 2 * rank], first[2 * rank]
    fwd_scale = lax.rsqrt(fwd_squares / D + epsilon)
    activated = gated(fwd_proj * fwd_scale[None])[0].astype(jnp.bfloat16)
    output = forward_in.astype(jnp.float32) + dot(activated, down_full, 0, 0)
    output = output.astype(jnp.bfloat16)
    middle = lax.axis_size("pipe") // 2
    act_next = lax.ppermute(output, "pipe", [(i - 1, i) for i in range(1, 2 * middle) if i != middle])
    return act_next, output, grad_act


def gathered(up_proj, down_proj):
    own_rank = down_proj.shape[0]
    weights = ring(jnp.concatenate([up_proj, down_proj]), "dp")
    return (
        jnp.concatenate([w[:own_rank] for w in weights]),
        jnp.concatenate([w[own_rank:] for w in weights]),
    )


def ahead(forward_in, cotangent, up_proj, down_proj, stash):
    own_rank, features = down_proj.shape
    near = near_sections(lax.axis_size("pipe"))
    last = lax.axis_size("pipe") - 1
    crossed = lax.ppermute(stash, "pipe", [(i, i ^ 1) for i in near])
    weights = spread(jnp.concatenate([up_proj, down_proj]), "dp")
    weights, cotangent_sent, crossed = lax.optimization_barrier((weights, cotangent, crossed))
    returned = lax.ppermute(crossed, "pipe", [(i ^ 1, last - i) for i in near])
    cotangents = spread(cotangent_sent, "dp")
    up_full = weights[:, :own_rank].reshape(-1, features)
    down_full = weights[:, own_rank:].reshape(-1, features)
    act_next, output, grad_act = staged("mp", forward, forward_in, cotangent, up_full, down_full)
    return act_next, output, grad_act, up_full, cotangents, returned


def backward(returned, cotangent, up_full, grad_act):
    rank = up_full.shape[0]
    second = jnp.concatenate([dot(up_full, returned, 1, 1), square_rows(returned)])
    second = summed(second.astype(jnp.bfloat16), "mp")
    back_proj, back_squares = second[:rank], second[rank]
    back_scale = lax.rsqrt(back_squares / D + epsilon)
    back_value, back_slope = gated(back_proj * back_scale[None])
    back_act = back_value.astype(jnp.bfloat16)
    grad_hidden = grad_act * back_slope
    grad_proj = (grad_hidden * back_scale[None]).astype(jnp.bfloat16)
    grad_scale = jnp.sum(grad_hidden * back_proj, axis=0)
    pull = -(back_scale**3) * grad_scale / D
    grad_input = cotangent.astype(jnp.float32) + dot(grad_proj, up_full, 0, 0)
    grad_input = grad_input + returned.astype(jnp.float32) * pull[:, None]
    up_terms = dot(grad_proj, returned, 1, 0).astype(jnp.bfloat16)
    terms = jnp.concatenate([up_terms, back_act], 1)
    return grad_input.astype(jnp.bfloat16), terms.reshape(lax.axis_size("dp"), -1, terms.shape[1])


def shards(act_in, grad_in, stash_far, up_proj, down_proj):
    forward_in = act_in[0]
    cotangent = grad_in[0]
    rows, features = cotangent.shape
    group = lax.axis_size("dp")
    sections = lax.axis_size("pipe")
    far = [i for i in range(sections) if i not in near_sections(sections)]
    returned = lax.ppermute(stash_far[0], "pipe", [(i, sections - 1 - i) for i in far])
    act_next, output, grad_act, up_full, cotangents, returned_near = staged(
        "dp", ahead, forward_in, cotangent, up_proj[0].T, down_proj[0], stash_far[0]
    )
    middle = sections // 2
    act_middle = lax.ppermute(output, "pipe", [(middle - 1, middle)])
    returned = returned + returned_near
    grad_input, terms = staged("dp", backward, returned, cotangent, up_full, grad_act)
    terms = lax.all_to_all(terms, "dp", split_axis=0, concat_axis=0, tiled=True)
    grad_prev = shifted(grad_input, "pipe", -1)
    up_grad = jnp.sum(terms[:, :, :features].astype(jnp.float32), axis=0)
    down_grad = lax.dot_general(
        terms[:, :, features:], cotangents, (((0, 2), (0, 1)), ((), ())), preferred_element_type=jnp.float32
    )
    return (
        (act_next + act_middle)[None],
        grad_prev[None],
        up_grad.astype(jnp.bfloat16).T[None],
        down_grad.astype(jnp.bfloat16)[None],
    )


def solution(mesh):
    in_specs = (
        P("pipe", "dp", "mp"),
        P("pipe", "dp", "mp"),
        P("pipe", "dp", "mp"),
        P("pipe", "mp", "dp"),
        P("pipe", "dp", "mp"),
    )
    out_specs = (
        P("pipe", "dp", "mp"),
        P("pipe", "dp", "mp"),
        P("pipe", "mp", "dp"),
        P("pipe", "dp", "mp"),
    )
    return jax.shard_map(shards, mesh=mesh, in_specs=in_specs, out_specs=out_specs, check_vma=False)
```

```python
import functools

import jax
import jax.numpy as jnp
from jax import lax
from jax.experimental import pallas as pl
from jax.experimental.pallas import tpu as pltpu
from jax.sharding import PartitionSpec as P

D = 12288


epsilon = 1e-05


TILE = 1024


EXTRA = 16


def shifted(block, axis, distance):
    devices = range(lax.axis_size(axis))
    route = [(i - distance, i) for i in devices if i - distance in devices]
    return lax.ppermute(block, axis, route)


def near_sections(count):
    planes = count // 2
    return [i for i in range(count) if min((2 * (i // 2) + 1) % planes, -(2 * (i // 2) + 1) % planes) <= 3]


def spread(block, axis):
    copies = jnp.broadcast_to(block[None], (lax.axis_size(axis),) + block.shape)
    return lax.all_to_all(copies, axis, split_axis=0, concat_axis=0, tiled=True)


def summed(block, axis):
    size, distance = lax.axis_size(axis), 1
    while distance < size:
        block = block + lax.ppermute(block, axis, [(i, i ^ distance) for i in range(size)])
        distance *= 2
    return block


def staged(axis, step, *args):
    shapes = jax.eval_shape(step, *args)
    empty = lambda *_: jax.tree.map(lambda leaf: jnp.zeros(leaf.shape, leaf.dtype), shapes)
    return lax.cond(lax.axis_index(axis) < lax.axis_size(axis), step, empty, *args)


def dot(left, right, left_dim, right_dim):
    return lax.dot_general(
        left, right, (((left_dim,), (right_dim,)), ((), ())), preferred_element_type=jnp.float32
    )


def gated(hidden):
    sigmoid_value = jax.nn.sigmoid(hidden)
    return (hidden * sigmoid_value, sigmoid_value * (1.0 + hidden * (1.0 - sigmoid_value)))


def call(kernel, name, args, out_shape, scratch, flops):
    in_vmem = pl.BlockSpec(memory_space=pltpu.VMEM)
    return pl.pallas_call(
        kernel,
        in_specs=[in_vmem] * len(args),
        out_specs=jax.tree.map(lambda _: in_vmem, out_shape),
        out_shape=out_shape,
        scratch_shapes=scratch,
        name=name,
        compiler_params=pltpu.CompilerParams(vmem_limit_bytes=24 * 2**20),
        cost_estimate=pl.CostEstimate(flops=flops, bytes_accessed=5 * 2**20, transcendentals=0),
    )(*args)


def struct(*shape, dtype=jnp.bfloat16):
    return jax.ShapeDtypeStruct(shape, dtype)


def tiles(features):
    return [pl.ds(start, TILE) for start in range(0, features, TILE)]


def up_rows(weights_ref, tile):
    group, own_rank, _ = weights_ref.shape
    own_rank //= 2
    return weights_ref[:, :own_rank, tile].reshape(group * own_rank, TILE)


def down_rows(weights_ref, tile):
    group, own_rank, _ = weights_ref.shape
    own_rank //= 2
    return weights_ref[:, own_rank:, tile].reshape(group * own_rank, TILE)


def squares_of(inputs):
    wide = inputs.astype(jnp.float32)
    return sum(jnp.square(wide[:, i : i + 128]) for i in range(0, wide.shape[1], 128))


def row_sums(squares):
    return jnp.broadcast_to(jnp.sum(squares.T, axis=0, keepdims=True), (EXTRA, squares.shape[0]))


def first_kernel(weights_ref, input_ref, cotangent_ref, out_ref):
    rank = (out_ref.shape[0] - EXTRA) // 2
    product = squares = grad_act = 0.0
    for tile in tiles(input_ref.shape[1]):
        inputs = input_ref[:, tile]
        product += dot(up_rows(weights_ref, tile), inputs, 1, 1)
        grad_act += dot(down_rows(weights_ref, tile), cotangent_ref[:, tile], 1, 1)
        squares += squares_of(inputs)
    out_ref[:rank, :] = product.astype(out_ref.dtype)
    out_ref[rank : 2 * rank, :] = grad_act.astype(out_ref.dtype)
    out_ref[2 * rank :, :] = row_sums(squares).astype(out_ref.dtype)


def first_products(weights, inputs, cotangent):
    group, own_rank, features = weights.shape
    rank, rows = group * own_rank // 2, inputs.shape[0]
    return call(
        first_kernel, "first_products", (weights, inputs, cotangent),
        struct(2 * rank + EXTRA, rows, dtype=jnp.float32), [], 4 * rank * rows * features,
    )


def second_kernel(up_ref, *refs):
    *input_refs, out_ref, sum_ref = refs
    rank = up_ref.shape[0]
    product = squares = 0.0
    for tile in tiles(up_ref.shape[1]):
        inputs = sum(ref[:, tile] for ref in input_refs)
        sum_ref[:, tile] = inputs
        product += dot(up_ref[:, tile], inputs, 1, 1)
        squares += squares_of(inputs)
    out_ref[:rank, :] = product.astype(out_ref.dtype)
    out_ref[rank:, :] = row_sums(squares).astype(out_ref.dtype)


def second_products(up_full, inputs):
    rank, features = up_full.shape
    rows = inputs[0].shape[0]
    return call(
        second_kernel, "second_products", (up_full, *inputs),
        [struct(rank + EXTRA, rows), struct(rows, features)], [], 2 * rank * rows * features,
    )


def output_kernel(parts_ref, weights_ref, input_ref, out_ref, grad_act_ref, up_ref):
    rank = grad_act_ref.shape[0]
    scale = lax.rsqrt(parts_ref[2 * rank : 2 * rank + 1, :] / D + epsilon)
    act = gated(parts_ref[:rank, :] * scale)[0].astype(jnp.bfloat16)
    grad_act_ref[...] = parts_ref[rank : 2 * rank, :]
    for tile in tiles(input_ref.shape[1]):
        out = input_ref[:, tile].astype(jnp.float32) + dot(act, down_rows(weights_ref, tile), 0, 0)
        out_ref[:, tile] = out.astype(out_ref.dtype)
        up_ref[:, tile] = up_rows(weights_ref, tile)


def forward_output(parts, weights, inputs):
    group, own_rank, features = weights.shape
    rank, rows = group * own_rank // 2, inputs.shape[0]
    return call(
        output_kernel, "forward_output", (parts, weights, inputs),
        [struct(*inputs.shape), struct(rank, rows, dtype=jnp.float32), struct(rank, features)],
        [], 2 * rank * rows * features,
    )


def input_kernel(parts_ref, grad_act_ref, up_ref, returned_ref, cotangent_ref, grad_ref, terms_ref):
    group, own_rank, _ = terms_ref.shape
    rank, rows = grad_act_ref.shape
    features = up_ref.shape[1]
    parts = jnp.sum(parts_ref[...].astype(jnp.float32), axis=0)
    back_proj = parts[:rank]
    scale = lax.rsqrt(parts[rank:] / D + epsilon)
    value, slope = gated(back_proj * scale[:1])
    grad_hidden = grad_act_ref[...] * slope
    proj = (grad_hidden * scale[:1]).astype(jnp.bfloat16)
    grad_scale = jnp.sum(grad_hidden * back_proj, axis=0, keepdims=True)
    pull = (-(scale * scale * scale) * grad_scale / D).T[:, :1]
    terms_ref[:, :, features:] = value.astype(terms_ref.dtype).reshape(group, own_rank, rows)
    for tile in tiles(features):
        returned = returned_ref[:, tile]
        grad = cotangent_ref[:, tile].astype(jnp.float32) + dot(proj, up_ref[:, tile], 0, 0)
        grad_ref[:, tile] = (grad + returned.astype(jnp.float32) * pull).astype(grad_ref.dtype)
        term = dot(proj, returned, 1, 0).astype(terms_ref.dtype)
        terms_ref[:, :, tile] = term.reshape(group, own_rank, TILE)


def input_gradient(parts, grad_act, up_full, returned, cotangent):
    rank, features = up_full.shape
    rows, group = returned.shape[0], lax.axis_size("dp")
    return call(
        input_kernel, "input_gradient", (parts, grad_act, up_full, returned, cotangent),
        [struct(rows, features), struct(group, rank // group, features + rows)], [], 4 * rank * rows * features,
    )


def weight_kernel(terms_ref, cotangents_ref, up_ref, down_ref):
    group, rows, features = cotangents_ref.shape
    acts = [terms_ref[k, :, features:] for k in range(group)]
    for tile in tiles(features):
        up_ref[:, tile] = jnp.sum(terms_ref[:, :, tile].astype(jnp.float32), axis=0).astype(up_ref.dtype)
        down = sum(dot(acts[k], cotangents_ref[k, :, tile], 1, 0) for k in range(group))
        down_ref[:, tile] = down.astype(down_ref.dtype)


def weight_gradients(terms, cotangents):
    group, rows, features = cotangents.shape
    share = (terms.shape[1], features)
    return call(
        weight_kernel, "weight_gradients", (terms, cotangents),
        [struct(*share)] * 2, [], 2 * group * rows * share[0] * features,
    )


def forward(weights, forward_in, cotangent):
    parts = summed(first_products(weights, forward_in, cotangent), "mp")
    output, grad_act, up_full = forward_output(parts, weights, forward_in)
    count = lax.axis_size("pipe")
    act_next = lax.ppermute(output, "pipe", [(i - 1, i) for i in range(1, count) if i != count // 2])
    return act_next, output, grad_act, up_full


def beside(weights, copies, forward_in, cotangent):
    cotangents = lax.all_to_all(copies, "dp", split_axis=0, concat_axis=0, tiled=True)
    return *staged("mp", forward, weights, forward_in, cotangent), cotangents


def ahead(forward_in, cotangent, up_proj, down_proj, stash):
    count, group = lax.axis_size("pipe"), lax.axis_size("dp")
    near = near_sections(count)
    copies = [jnp.broadcast_to(w[None], (group,) + w.shape) for w in (up_proj, down_proj)]
    weights = lax.all_to_all(jnp.concatenate(copies, 1), "dp", split_axis=0, concat_axis=0, tiled=True)
    crossed = lax.ppermute(stash, "pipe", [(i, i ^ 1) for i in near])
    copies = jnp.broadcast_to(cotangent[None], (group,) + cotangent.shape)
    copies, crossed = lax.optimization_barrier((copies, crossed))
    returned_far = lax.ppermute(stash, "pipe", [(i, count - 1 - i) for i in range(count // 2) if i not in near])
    returned_near = lax.ppermute(crossed, "pipe", [(i ^ 1, count - 1 - i) for i in near])
    act_next, output, grad_act, up_full, cotangents = staged("mp", beside, weights, copies, forward_in, cotangent)
    return act_next, output, grad_act, up_full, cotangents, returned_far, returned_near


def backward(returned, cotangent, up_full, grad_act):
    parts, returned = second_products(up_full, returned)
    return input_gradient(spread(parts, "mp"), grad_act, up_full, returned, cotangent)


def last_terms(terms, cotangents, act_next, output):
    middle = lax.axis_size("pipe") // 2
    act_middle = lax.ppermute(output, "pipe", [(middle - 1, middle)])
    terms = lax.all_to_all(terms, "dp", split_axis=0, concat_axis=0, tiled=True)
    return *weight_gradients(terms, cotangents), act_next + act_middle


def shards(act_in, grad_in, stash_far, up_proj, down_proj):
    cotangent = grad_in[0]
    count = lax.axis_size("pipe")
    near = near_sections(count)
    returned = lax.ppermute(
        stash_far[0], "pipe", [(i, count - 1 - i) for i in range(count // 2, count) if i not in near]
    )
    act_next, output, grad_act, up_full, cotangents, *returned_later = staged(
        "dp", ahead, act_in[0], cotangent, up_proj[0].T, down_proj[0], stash_far[0]
    )
    grad_input, terms = staged("dp", backward, [returned, *returned_later], cotangent, up_full, grad_act)
    grad_prev = shifted(grad_input, "pipe", -1)
    up_grad, down_grad, act_next = staged("dp", last_terms, terms, cotangents, act_next, output)
    return act_next[None], grad_prev[None], up_grad.T[None], down_grad[None]


def solution(mesh):
    in_specs = (
        P("pipe", "dp", "mp"),
        P("pipe", "dp", "mp"),
        P("pipe", "dp", "mp"),
        P("pipe", "mp", "dp"),
        P("pipe", "dp", "mp"),
    )
    out_specs = (
        P("pipe", "dp", "mp"),
        P("pipe", "dp", "mp"),
        P("pipe", "mp", "dp"),
        P("pipe", "dp", "mp"),
    )
    return jax.shard_map(shards, mesh=mesh, in_specs=in_specs, out_specs=out_specs, check_vma=False)
```

```python
import functools

import jax
import jax.numpy as jnp
from jax import lax
from jax.experimental import pallas as pl
from jax.experimental.pallas import tpu as pltpu
from jax.sharding import PartitionSpec as P

D = 12288


epsilon = 1e-05


TILE = 1024


EXTRA = 16


def shifted(block, axis, distance):
    devices = range(lax.axis_size(axis))
    route = [(i - distance, i) for i in devices if i - distance in devices]
    return lax.ppermute(block, axis, route)


def stash_routes(count):
    planes, middle = count // 2, count // 2
    near = [i for i in range(count) if min((2 * (i // 2) + 1) % planes, -(2 * (i // 2) + 1) % planes) <= 3]
    below = [middle - 2, middle - 1]
    first = [i for i in range(middle, count) if i not in near] + below
    second = [i for i in range(middle) if i not in near]
    crossing = [i for i in near if i not in below]
    return [[(i, count - 1 - i) for i in sources] for sources in (first, second, crossing)]


def spread(block, axis):
    copies = jnp.broadcast_to(block[None], (lax.axis_size(axis),) + block.shape)
    return lax.all_to_all(copies, axis, split_axis=0, concat_axis=0, tiled=True)


def summed(block, axis):
    size, distance = lax.axis_size(axis), 1
    while distance < size:
        block = block + lax.ppermute(block, axis, [(i, i ^ distance) for i in range(size)])
        distance *= 2
    return block


def staged(axis, step, *args):
    shapes = jax.eval_shape(step, *args)
    empty = lambda *_: jax.tree.map(lambda leaf: jnp.zeros(leaf.shape, leaf.dtype), shapes)
    return lax.cond(lax.axis_index(axis) < lax.axis_size(axis), step, empty, *args)


def dot(left, right, left_dim, right_dim):
    return lax.dot_general(
        left, right, (((left_dim,), (right_dim,)), ((), ())), preferred_element_type=jnp.float32
    )


def gated(hidden):
    sigmoid_value = jax.nn.sigmoid(hidden)
    return (hidden * sigmoid_value, sigmoid_value * (1.0 + hidden * (1.0 - sigmoid_value)))


def call(kernel, name, args, out_shape, scratch, flops, fetched=()):
    in_vmem = pl.BlockSpec(memory_space=pltpu.VMEM)
    anywhere = pl.BlockSpec(memory_space=pl.ANY)
    return pl.pallas_call(
        kernel,
        in_specs=[anywhere if i in fetched else in_vmem for i in range(len(args))],
        out_specs=jax.tree.map(lambda _: in_vmem, out_shape),
        out_shape=out_shape,
        scratch_shapes=scratch,
        name=name,
        compiler_params=pltpu.CompilerParams(vmem_limit_bytes=24 * 2**20),
        cost_estimate=pl.CostEstimate(flops=flops, bytes_accessed=5 * 2**20, transcendentals=0),
    )(*args)


def struct(*shape, dtype=jnp.bfloat16):
    return jax.ShapeDtypeStruct(shape, dtype)


def tiles(features):
    return [pl.ds(start, TILE) for start in range(0, features, TILE)]


def up_rows(weights_ref, tile):
    group, own_rank, _ = weights_ref.shape
    own_rank //= 2
    return weights_ref[:, :own_rank, tile].reshape(group * own_rank, TILE)


def down_rows(weights_ref, tile):
    group, own_rank, _ = weights_ref.shape
    own_rank //= 2
    return weights_ref[:, own_rank:, tile].reshape(group * own_rank, TILE)


def squares_of(inputs):
    wide = inputs.astype(jnp.float32)
    return sum(jnp.square(wide[:, i : i + 128]) for i in range(0, wide.shape[1], 128))


def row_sums(squares):
    return jnp.broadcast_to(jnp.sum(squares.T, axis=0, keepdims=True), (EXTRA, squares.shape[0]))


def first_kernel(weights_ref, input_ref, cotangent_ref, out_ref):
    rank = (out_ref.shape[0] - EXTRA) // 2
    product = squares = grad_act = 0.0
    for tile in tiles(input_ref.shape[1]):
        inputs = input_ref[:, tile]
        product += dot(up_rows(weights_ref, tile), inputs, 1, 1)
        grad_act += dot(down_rows(weights_ref, tile), cotangent_ref[:, tile], 1, 1)
        squares += squares_of(inputs)
    out_ref[:rank, :] = product.astype(out_ref.dtype)
    out_ref[rank : 2 * rank, :] = grad_act.astype(out_ref.dtype)
    out_ref[2 * rank :, :] = row_sums(squares).astype(out_ref.dtype)


def first_products(weights, inputs, cotangent):
    group, own_rank, features = weights.shape
    rank, rows = group * own_rank // 2, inputs.shape[0]
    return call(
        first_kernel, "first_products", (weights, inputs, cotangent),
        struct(2 * rank + EXTRA, rows, dtype=jnp.float32), [], 4 * rank * rows * features,
    )


def second_kernel(up_hbm, first_ref, second_ref, crossed_ref, out_ref, returned_ref, up_ref, done):
    rank, features = up_ref.shape
    section = lax.axis_index("pipe")
    kind = 0
    for k, routes in enumerate(stash_routes(lax.axis_size("pipe"))):
        kind += k * sum((section == target).astype(jnp.int32) for _, target in routes)

    def up_copy(k, tile):
        return pltpu.make_async_copy(up_hbm.at[:, tile], up_ref.at[:, tile], done.at[0, k])

    def returned_copy(ref, k, tile):
        return pltpu.make_async_copy(ref.at[:, tile], returned_ref.at[:, tile], done.at[1, k])

    for k, tile in enumerate(tiles(features)):
        up_copy(k, tile).start()
        for i, ref in enumerate((first_ref, second_ref, crossed_ref)):

            @pl.when(kind == i)
            def _(ref=ref, k=k, tile=tile):
                returned_copy(ref, k, tile).start()

    product = squares = 0.0
    for k, tile in enumerate(tiles(features)):
        up_copy(k, tile).wait()
        returned_copy(first_ref, k, tile).wait()
        inputs = returned_ref[:, tile]
        product += dot(up_ref[:, tile], inputs, 1, 1)
        squares += squares_of(inputs)
    out_ref[:rank, :] = product.astype(out_ref.dtype)
    out_ref[rank:, :] = row_sums(squares).astype(out_ref.dtype)


def second_products(up_full, inputs):
    rank, features = up_full.shape
    rows = inputs[0].shape[0]
    return call(
        second_kernel, "second_products", (up_full, *inputs),
        [struct(rank + EXTRA, rows), struct(rows, features)],
        [pltpu.VMEM(up_full.shape, jnp.bfloat16), pltpu.SemaphoreType.DMA((2, features // TILE))],
        2 * rank * rows * features, (0, 1, 2, 3),
    )


def output_kernel(parts_ref, weights_ref, input_ref, out_ref, grad_act_ref, up_ref):
    rank = grad_act_ref.shape[0]
    scale = lax.rsqrt(parts_ref[2 * rank : 2 * rank + 1, :] / D + epsilon)
    act = gated(parts_ref[:rank, :] * scale)[0].astype(jnp.bfloat16)
    grad_act_ref[...] = parts_ref[rank : 2 * rank, :]
    for tile in tiles(input_ref.shape[1]):
        out = input_ref[:, tile].astype(jnp.float32) + dot(act, down_rows(weights_ref, tile), 0, 0)
        out_ref[:, tile] = out.astype(out_ref.dtype)
        up_ref[:, tile] = up_rows(weights_ref, tile)


def forward_output(parts, weights, inputs):
    group, own_rank, features = weights.shape
    rank, rows = group * own_rank // 2, inputs.shape[0]
    return call(
        output_kernel, "forward_output", (parts, weights, inputs),
        [struct(*inputs.shape), struct(rank, rows, dtype=jnp.float32), struct(rank, features)],
        [], 2 * rank * rows * features,
    )


def input_kernel(parts_ref, grad_act_ref, up_ref, returned_ref, cotangent_ref, grad_ref, terms_ref):
    group, own_rank, _ = terms_ref.shape
    rank, rows = grad_act_ref.shape
    features = up_ref.shape[1]
    parts = jnp.sum(parts_ref[...].astype(jnp.float32), axis=0)
    back_proj = parts[:rank]
    scale = lax.rsqrt(parts[rank:] / D + epsilon)
    value, slope = gated(back_proj * scale[:1])
    grad_hidden = grad_act_ref[...] * slope
    proj = (grad_hidden * scale[:1]).astype(jnp.bfloat16)
    grad_scale = jnp.sum(grad_hidden * back_proj, axis=0, keepdims=True)
    pull = (-(scale * scale * scale) * grad_scale / D).T[:, :1]
    terms_ref[:, :, features:] = value.astype(terms_ref.dtype).reshape(group, own_rank, rows)
    for tile in tiles(features):
        returned = returned_ref[:, tile]
        grad = cotangent_ref[:, tile].astype(jnp.float32) + dot(proj, up_ref[:, tile], 0, 0)
        grad_ref[:, tile] = (grad + returned.astype(jnp.float32) * pull).astype(grad_ref.dtype)
        term = dot(proj, returned, 1, 0).astype(terms_ref.dtype)
        terms_ref[:, :, tile] = term.reshape(group, own_rank, TILE)


def input_gradient(parts, grad_act, up_full, returned, cotangent):
    rank, features = up_full.shape
    rows, group = returned.shape[0], lax.axis_size("dp")
    return call(
        input_kernel, "input_gradient", (parts, grad_act, up_full, returned, cotangent),
        [struct(rows, features), struct(group, rank // group, features + rows)], [], 4 * rank * rows * features,
    )


def weight_kernel(terms_ref, cotangents_ref, up_ref, down_ref):
    group, rows, features = cotangents_ref.shape
    acts = [terms_ref[k, :, features:] for k in range(group)]
    for tile in tiles(features):
        up_ref[:, tile] = jnp.sum(terms_ref[:, :, tile].astype(jnp.float32), axis=0).astype(up_ref.dtype)
        down = sum(dot(acts[k], cotangents_ref[k, :, tile], 1, 0) for k in range(group))
        down_ref[:, tile] = down.astype(down_ref.dtype)


def weight_gradients(terms, cotangents):
    group, rows, features = cotangents.shape
    share = (terms.shape[1], features)
    return call(
        weight_kernel, "weight_gradients", (terms, cotangents),
        [struct(*share)] * 2, [], 2 * group * rows * share[0] * features,
    )


def forward(weights, forward_in, cotangent):
    parts = summed(first_products(weights, forward_in, cotangent), "mp")
    output, grad_act, up_full = forward_output(parts, weights, forward_in)
    return shifted(output, "pipe", 1), grad_act, up_full


def beside(weights, copies, forward_in, cotangent):
    cotangents = lax.all_to_all(copies, "dp", split_axis=0, concat_axis=0, tiled=True)
    return *staged("mp", forward, weights, forward_in, cotangent), cotangents


def ahead(forward_in, cotangent, up_proj, down_proj, stash):
    group = lax.axis_size("dp")
    _, second, crossing = stash_routes(lax.axis_size("pipe"))
    copies = [jnp.broadcast_to(w[None], (group,) + w.shape) for w in (up_proj, down_proj)]
    weights = lax.all_to_all(jnp.concatenate(copies, 1), "dp", split_axis=0, concat_axis=0, tiled=True)
    crossed = lax.ppermute(stash, "pipe", [(i, i ^ 1) for i, _ in crossing])
    copies = jnp.broadcast_to(cotangent[None], (group,) + cotangent.shape)
    copies, crossed = lax.optimization_barrier((copies, crossed))
    returned_second = lax.ppermute(stash, "pipe", second)
    returned_crossed = lax.ppermute(crossed, "pipe", [(i ^ 1, target) for i, target in crossing])
    act_next, grad_act, up_full, cotangents = staged("mp", beside, weights, copies, forward_in, cotangent)
    return act_next, grad_act, up_full, cotangents, returned_second, returned_crossed


def backward(returned, cotangent, up_full, grad_act):
    parts, returned = second_products(up_full, returned)
    return input_gradient(spread(parts, "mp"), grad_act, up_full, returned, cotangent)


def hold_kernel(source_ref, out_ref):
    out_ref[...] = source_ref[...]


def held(block):
    return call(hold_kernel, "held", (block,), struct(*block.shape), [], 0)


def last_terms(terms, cotangents, act_next):
    terms = lax.all_to_all(terms, "dp", split_axis=0, concat_axis=0, tiled=True)
    return *weight_gradients(terms, cotangents), held(act_next)


def shards(act_in, grad_in, stash_far, up_proj, down_proj):
    cotangent = grad_in[0]
    first = stash_routes(lax.axis_size("pipe"))[0]
    returned = lax.ppermute(stash_far[0], "pipe", first)
    act_next, grad_act, up_full, cotangents, *returned_later = staged(
        "dp", ahead, act_in[0], cotangent, up_proj[0].T, down_proj[0], stash_far[0]
    )
    grad_input, terms = staged("dp", backward, [returned, *returned_later], cotangent, up_full, grad_act)
    grad_prev = shifted(grad_input, "pipe", -1)
    up_grad, down_grad, act_next = staged("dp", last_terms, terms, cotangents, act_next)
    return act_next[None], grad_prev[None], up_grad.T[None], down_grad[None]


def solution(mesh):
    in_specs = (
        P("pipe", "dp", "mp"),
        P("pipe", "dp", "mp"),
        P("pipe", "dp", "mp"),
        P("pipe", "mp", "dp"),
        P("pipe", "dp", "mp"),
    )
    out_specs = (
        P("pipe", "dp", "mp"),
        P("pipe", "dp", "mp"),
        P("pipe", "mp", "dp"),
        P("pipe", "dp", "mp"),
    )
    return jax.shard_map(shards, mesh=mesh, in_specs=in_specs, out_specs=out_specs, check_vma=False)
```

```python
import functools

import jax
import jax.numpy as jnp
from jax import lax
from jax.experimental import pallas as pl
from jax.experimental.pallas import tpu as pltpu
from jax.sharding import PartitionSpec as P

D = 12288


epsilon = 1e-05


TILE = 1024


EXTRA = 16


def shifted(block, axis, distance):
    devices = range(lax.axis_size(axis))
    route = [(i - distance, i) for i in devices if i - distance in devices]
    return lax.ppermute(block, axis, route)


def stash_routes(count):
    planes, middle = count // 2, count // 2
    near = [i for i in range(count) if min((2 * (i // 2) + 1) % planes, -(2 * (i // 2) + 1) % planes) <= 3]
    below = [middle - 2, middle - 1]
    wrapping = list(range(count // 4 - 2, count // 4 + 2))
    first = [i for i in range(middle, count) if i not in near] + below + wrapping
    second = [i for i in range(middle) if i not in near + wrapping]
    crossing = [i for i in near if i not in below]
    return [[(i, count - 1 - i) for i in sources] for sources in (first, second, crossing)]


def spread(block, axis):
    copies = jnp.broadcast_to(block[None], (lax.axis_size(axis),) + block.shape)
    return lax.all_to_all(copies, axis, split_axis=0, concat_axis=0, tiled=True)


def summed(block, axis):
    size, distance = lax.axis_size(axis), 1
    while distance < size:
        block = block.astype(jnp.bfloat16) if 2 * distance == size else block
        far = lax.ppermute(block, axis, [(i, i ^ distance) for i in range(size)])
        block = block.astype(jnp.float32) + far.astype(jnp.float32)
        distance *= 2
    return block


def staged(axis, step, *args):
    shapes = jax.eval_shape(step, *args)
    empty = lambda *_: jax.tree.map(lambda leaf: jnp.zeros(leaf.shape, leaf.dtype), shapes)
    return lax.cond(lax.axis_index(axis) < lax.axis_size(axis), step, empty, *args)


def dot(left, right, left_dim, right_dim):
    return lax.dot_general(
        left, right, (((left_dim,), (right_dim,)), ((), ())), preferred_element_type=jnp.float32
    )


def gated(hidden):
    sigmoid_value = jax.nn.sigmoid(hidden)
    return (hidden * sigmoid_value, sigmoid_value * (1.0 + hidden * (1.0 - sigmoid_value)))


def call(kernel, name, args, out_shape, scratch, flops, fetched=()):
    in_vmem = pl.BlockSpec(memory_space=pltpu.VMEM)
    anywhere = pl.BlockSpec(memory_space=pl.ANY)
    return pl.pallas_call(
        kernel,
        in_specs=[anywhere if i in fetched else in_vmem for i in range(len(args))],
        out_specs=jax.tree.map(lambda _: in_vmem, out_shape),
        out_shape=out_shape,
        scratch_shapes=scratch,
        name=name,
        compiler_params=pltpu.CompilerParams(vmem_limit_bytes=24 * 2**20),
        cost_estimate=pl.CostEstimate(flops=flops, bytes_accessed=5 * 2**20, transcendentals=0),
    )(*args)


def struct(*shape, dtype=jnp.bfloat16):
    return jax.ShapeDtypeStruct(shape, dtype)


def tiles(features):
    return [pl.ds(start, TILE) for start in range(0, features, TILE)]


def up_rows(weights_ref, tile):
    group, own_rank, _ = weights_ref.shape
    own_rank //= 2
    return weights_ref[:, :own_rank, tile].reshape(group * own_rank, TILE)


def down_rows(weights_ref, tile):
    group, own_rank, _ = weights_ref.shape
    own_rank //= 2
    return weights_ref[:, own_rank:, tile].reshape(group * own_rank, TILE)


def squares_of(inputs):
    wide = inputs.astype(jnp.float32)
    return sum(jnp.square(wide[:, i : i + 128]) for i in range(0, wide.shape[1], 128))


def row_sums(squares):
    return jnp.broadcast_to(jnp.sum(squares.T, axis=0, keepdims=True), (EXTRA, squares.shape[0]))


def first_kernel(weights_ref, input_ref, cotangent_ref, out_ref):
    rank = (out_ref.shape[0] - EXTRA) // 2
    product = squares = grad_act = 0.0
    for tile in tiles(input_ref.shape[1]):
        inputs = input_ref[:, tile]
        product += dot(up_rows(weights_ref, tile), inputs, 1, 1)
        grad_act += dot(down_rows(weights_ref, tile), cotangent_ref[:, tile], 1, 1)
        squares += squares_of(inputs)
    out_ref[:rank, :] = product.astype(out_ref.dtype)
    out_ref[rank : 2 * rank, :] = grad_act.astype(out_ref.dtype)
    out_ref[2 * rank :, :] = row_sums(squares).astype(out_ref.dtype)


def first_products(weights, inputs, cotangent):
    group, own_rank, features = weights.shape
    rank, rows = group * own_rank // 2, inputs.shape[0]
    return call(
        first_kernel, "first_products", (weights, inputs, cotangent),
        struct(2 * rank + EXTRA, rows, dtype=jnp.float32), [], 4 * rank * rows * features,
    )


def second_kernel(up_hbm, first_ref, second_ref, crossed_ref, out_ref, returned_ref, up_ref, done):
    rank, features = up_ref.shape
    section = lax.axis_index("pipe")
    kind = 0
    for k, routes in enumerate(stash_routes(lax.axis_size("pipe"))):
        kind += k * sum((section == target).astype(jnp.int32) for _, target in routes)

    def up_copy(k, tile):
        return pltpu.make_async_copy(up_hbm.at[:, tile], up_ref.at[:, tile], done.at[0, k])

    def returned_copy(ref, k, tile):
        return pltpu.make_async_copy(ref.at[:, tile], returned_ref.at[:, tile], done.at[1, k])

    for k, tile in enumerate(tiles(features)):
        up_copy(k, tile).start()
        for i, ref in enumerate((first_ref, second_ref, crossed_ref)):

            @pl.when(kind == i)
            def _(ref=ref, k=k, tile=tile):
                returned_copy(ref, k, tile).start()

    product = squares = 0.0
    for k, tile in enumerate(tiles(features)):
        up_copy(k, tile).wait()
        returned_copy(first_ref, k, tile).wait()
        inputs = returned_ref[:, tile]
        product += dot(up_ref[:, tile], inputs, 1, 1)
        squares += squares_of(inputs)
    out_ref[:rank, :] = product.astype(out_ref.dtype)
    out_ref[rank:, :] = row_sums(squares).astype(out_ref.dtype)


def second_products(up_full, inputs):
    rank, features = up_full.shape
    rows = inputs[0].shape[0]
    return call(
        second_kernel, "second_products", (up_full, *inputs),
        [struct(rank + EXTRA, rows), struct(rows, features)],
        [pltpu.VMEM(up_full.shape, jnp.bfloat16), pltpu.SemaphoreType.DMA((2, features // TILE))],
        2 * rank * rows * features, (0, 1, 2, 3),
    )


def output_kernel(parts_ref, weights_ref, input_ref, out_ref, grad_act_ref, up_ref):
    rank = grad_act_ref.shape[0]
    scale = lax.rsqrt(parts_ref[2 * rank : 2 * rank + 1, :] / D + epsilon)
    act = gated(parts_ref[:rank, :] * scale)[0].astype(jnp.bfloat16)
    grad_act_ref[...] = parts_ref[rank : 2 * rank, :]
    for tile in tiles(input_ref.shape[1]):
        out = input_ref[:, tile].astype(jnp.float32) + dot(act, down_rows(weights_ref, tile), 0, 0)
        out_ref[:, tile] = out.astype(out_ref.dtype)
        up_ref[:, tile] = up_rows(weights_ref, tile)


def forward_output(parts, weights, inputs):
    group, own_rank, features = weights.shape
    rank, rows = group * own_rank // 2, inputs.shape[0]
    return call(
        output_kernel, "forward_output", (parts, weights, inputs),
        [struct(*inputs.shape), struct(rank, rows, dtype=jnp.float32), struct(rank, features)],
        [], 2 * rank * rows * features,
    )


def input_kernel(parts_ref, grad_act_ref, up_ref, returned_ref, cotangent_ref, grad_ref, terms_ref):
    group, own_rank, _ = terms_ref.shape
    rank, rows = grad_act_ref.shape
    features = up_ref.shape[1]
    parts = jnp.sum(parts_ref[...].astype(jnp.float32), axis=0)
    back_proj = parts[:rank]
    scale = lax.rsqrt(parts[rank:] / D + epsilon)
    value, slope = gated(back_proj * scale[:1])
    grad_hidden = grad_act_ref[...] * slope
    proj = (grad_hidden * scale[:1]).astype(jnp.bfloat16)
    grad_scale = jnp.sum(grad_hidden * back_proj, axis=0, keepdims=True)
    pull = (-(scale * scale * scale) * grad_scale / D).T[:, :1]
    terms_ref[:, :, features:] = value.astype(terms_ref.dtype).reshape(group, own_rank, rows)
    for tile in tiles(features):
        returned = returned_ref[:, tile]
        grad = cotangent_ref[:, tile].astype(jnp.float32) + dot(proj, up_ref[:, tile], 0, 0)
        grad_ref[:, tile] = (grad + returned.astype(jnp.float32) * pull).astype(grad_ref.dtype)
        term = dot(proj, returned, 1, 0).astype(terms_ref.dtype)
        terms_ref[:, :, tile] = term.reshape(group, own_rank, TILE)


def input_gradient(parts, grad_act, up_full, returned, cotangent):
    rank, features = up_full.shape
    rows, group = returned.shape[0], lax.axis_size("dp")
    return call(
        input_kernel, "input_gradient", (parts, grad_act, up_full, returned, cotangent),
        [struct(rows, features), struct(group, rank // group, features + rows)], [], 4 * rank * rows * features,
    )


def weight_kernel(terms_ref, cotangents_ref, up_ref, down_ref):
    group, rows, features = cotangents_ref.shape
    acts = [terms_ref[k, :, features:] for k in range(group)]
    for tile in tiles(features):
        up_ref[:, tile] = jnp.sum(terms_ref[:, :, tile].astype(jnp.float32), axis=0).astype(up_ref.dtype)
        down = sum(dot(acts[k], cotangents_ref[k, :, tile], 1, 0) for k in range(group))
        down_ref[:, tile] = down.astype(down_ref.dtype)


def weight_gradients(terms, cotangents):
    group, rows, features = cotangents.shape
    share = (terms.shape[1], features)
    return call(
        weight_kernel, "weight_gradients", (terms, cotangents),
        [struct(*share)] * 2, [], 2 * group * rows * share[0] * features,
    )


def forward(weights, forward_in, cotangent):
    parts = summed(first_products(weights, forward_in, cotangent), "mp")
    output, grad_act, up_full = forward_output(parts, weights, forward_in)
    return shifted(output, "pipe", 1), grad_act, up_full


def beside(weights, copies, forward_in, cotangent):
    cotangents = lax.all_to_all(copies, "dp", split_axis=0, concat_axis=0, tiled=True)
    return *staged("mp", forward, weights, forward_in, cotangent), cotangents


def ahead(forward_in, cotangent, up_proj, down_proj, stash):
    group = lax.axis_size("dp")
    _, second, crossing = stash_routes(lax.axis_size("pipe"))
    copies = [jnp.broadcast_to(w[None], (group,) + w.shape) for w in (up_proj, down_proj)]
    weights = lax.all_to_all(jnp.concatenate(copies, 1), "dp", split_axis=0, concat_axis=0, tiled=True)
    crossed = lax.ppermute(stash, "pipe", [(i, i ^ 1) for i, _ in crossing])
    copies = jnp.broadcast_to(cotangent[None], (group,) + cotangent.shape)
    copies, crossed = lax.optimization_barrier((copies, crossed))
    returned_second = lax.ppermute(stash, "pipe", second)
    returned_crossed = lax.ppermute(crossed, "pipe", [(i ^ 1, target) for i, target in crossing])
    act_next, grad_act, up_full, cotangents = staged("mp", beside, weights, copies, forward_in, cotangent)
    return act_next, grad_act, up_full, cotangents, returned_second, returned_crossed


def backward(returned, cotangent, up_full, grad_act):
    parts, returned = second_products(up_full, returned)
    return input_gradient(spread(parts, "mp"), grad_act, up_full, returned, cotangent)


def hold_kernel(source_ref, out_ref):
    out_ref[...] = source_ref[...]


def held(block):
    return call(hold_kernel, "held", (block,), struct(*block.shape), [], 0)


def last_terms(terms, cotangents, act_next):
    terms = lax.all_to_all(terms, "dp", split_axis=0, concat_axis=0, tiled=True)
    return *weight_gradients(terms, cotangents), held(act_next)


def shards(act_in, grad_in, stash_far, up_proj, down_proj):
    cotangent = grad_in[0]
    first = stash_routes(lax.axis_size("pipe"))[0]
    returned = lax.ppermute(stash_far[0], "pipe", first)
    act_next, grad_act, up_full, cotangents, *returned_later = staged(
        "dp", ahead, act_in[0], cotangent, up_proj[0].T, down_proj[0], stash_far[0]
    )
    grad_input, terms = staged("dp", backward, [returned, *returned_later], cotangent, up_full, grad_act)
    grad_prev = shifted(grad_input, "pipe", -1)
    up_grad, down_grad, act_next = staged("dp", last_terms, terms, cotangents, act_next)
    return act_next[None], grad_prev[None], up_grad.T[None], down_grad[None]


def solution(mesh):
    in_specs = (
        P("pipe", "dp", "mp"),
        P("pipe", "dp", "mp"),
        P("pipe", "dp", "mp"),
        P("pipe", "mp", "dp"),
        P("pipe", "dp", "mp"),
    )
    out_specs = (
        P("pipe", "dp", "mp"),
        P("pipe", "dp", "mp"),
        P("pipe", "mp", "dp"),
        P("pipe", "dp", "mp"),
    )
    return jax.shard_map(shards, mesh=mesh, in_specs=in_specs, out_specs=out_specs, check_vma=False)
```

```python
import functools

import jax
import jax.numpy as jnp
from jax import lax
from jax.experimental import pallas as pl
from jax.experimental.pallas import tpu as pltpu
from jax.sharding import PartitionSpec as P

D = 12288


epsilon = 1e-05


TILE = 1024


EXTRA = 16


def shifted(block, axis, distance):
    devices = range(lax.axis_size(axis))
    route = [(i - distance, i) for i in devices if i - distance in devices]
    return lax.ppermute(block, axis, route)


def stash_routes(count):
    planes, middle = count // 2, count // 2
    near = [i for i in range(count) if min((2 * (i // 2) + 1) % planes, -(2 * (i // 2) + 1) % planes) <= 3]
    below = [middle - 2, middle - 1]
    wrapping = list(range(count // 4 - 2, count // 4 + 2))
    first = [i for i in range(middle, count) if i not in near] + below + wrapping
    second = [i for i in range(middle) if i not in near + wrapping]
    crossing = [i for i in near if i not in below]
    return [[(i, count - 1 - i) for i in sources] for sources in (first, second, crossing)]


def spread(block, axis):
    copies = jnp.broadcast_to(block[None], (lax.axis_size(axis),) + block.shape)
    return lax.all_to_all(copies, axis, split_axis=0, concat_axis=0, tiled=True)


def summed(block, axis):
    size, distance = lax.axis_size(axis), 1
    while distance < size:
        block = block.astype(jnp.bfloat16) if 2 * distance == size else block
        far = lax.ppermute(block, axis, [(i, i ^ distance) for i in range(size)])
        block = block.astype(jnp.float32) + far.astype(jnp.float32)
        distance *= 2
    return block


def staged(axis, step, *args):
    shapes = jax.eval_shape(step, *args)
    empty = lambda *_: jax.tree.map(lambda leaf: jnp.zeros(leaf.shape, leaf.dtype), shapes)
    return lax.cond(lax.axis_index(axis) < lax.axis_size(axis), step, empty, *args)


def dot(left, right, left_dim, right_dim):
    return lax.dot_general(
        left, right, (((left_dim,), (right_dim,)), ((), ())), preferred_element_type=jnp.float32
    )


def gated(hidden):
    sigmoid_value = jax.nn.sigmoid(hidden)
    return (hidden * sigmoid_value, sigmoid_value * (1.0 + hidden * (1.0 - sigmoid_value)))


def call(kernel, name, args, out_shape, scratch, flops, fetched=()):
    in_vmem = pl.BlockSpec(memory_space=pltpu.VMEM)
    anywhere = pl.BlockSpec(memory_space=pl.ANY)
    return pl.pallas_call(
        kernel,
        in_specs=[anywhere if i in fetched else in_vmem for i in range(len(args))],
        out_specs=jax.tree.map(lambda _: in_vmem, out_shape),
        out_shape=out_shape,
        scratch_shapes=scratch,
        name=name,
        compiler_params=pltpu.CompilerParams(vmem_limit_bytes=24 * 2**20),
        cost_estimate=pl.CostEstimate(flops=flops, bytes_accessed=5 * 2**20, transcendentals=0),
    )(*args)


def struct(*shape, dtype=jnp.bfloat16):
    return jax.ShapeDtypeStruct(shape, dtype)


def tiles(features):
    return [pl.ds(start, TILE) for start in range(0, features, TILE)]


def up_rows(weights_ref, tile):
    group, own_rank, _ = weights_ref.shape
    own_rank //= 2
    return weights_ref[:, :own_rank, tile].reshape(group * own_rank, TILE)


def down_rows(weights_ref, tile):
    group, own_rank, _ = weights_ref.shape
    own_rank //= 2
    return weights_ref[:, own_rank:, tile].reshape(group * own_rank, TILE)


def squares_of(inputs):
    wide = inputs.astype(jnp.float32)
    return sum(jnp.square(wide[:, i : i + 128]) for i in range(0, wide.shape[1], 128))


def row_sums(squares):
    return jnp.broadcast_to(jnp.sum(squares.T, axis=0, keepdims=True), (EXTRA, squares.shape[0]))


def first_kernel(weights_ref, input_ref, out_ref):
    rank = out_ref.shape[0] - EXTRA
    product = squares = 0.0
    for tile in tiles(input_ref.shape[1]):
        inputs = input_ref[:, tile]
        product += dot(up_rows(weights_ref, tile), inputs, 1, 1)
        squares += squares_of(inputs)
    out_ref[:rank, :] = product.astype(out_ref.dtype)
    out_ref[rank:, :] = row_sums(squares).astype(out_ref.dtype)


def first_products(weights, inputs):
    group, own_rank, features = weights.shape
    rank, rows = group * own_rank // 2, inputs.shape[0]
    return call(
        first_kernel, "first_products", (weights, inputs),
        struct(rank + EXTRA, rows, dtype=jnp.float32), [], 2 * rank * rows * features,
    )


def second_kernel(up_hbm, first_ref, second_ref, crossed_ref, out_ref, returned_ref, up_ref, done):
    rank, features = up_ref.shape
    section = lax.axis_index("pipe")
    kind = 0
    for k, routes in enumerate(stash_routes(lax.axis_size("pipe"))):
        kind += k * sum((section == target).astype(jnp.int32) for _, target in routes)

    def up_copy(k, tile):
        return pltpu.make_async_copy(up_hbm.at[:, tile], up_ref.at[:, tile], done.at[0, k])

    def returned_copy(ref, k, tile):
        return pltpu.make_async_copy(ref.at[:, tile], returned_ref.at[:, tile], done.at[1, k])

    for k, tile in enumerate(tiles(features)):
        up_copy(k, tile).start()
        for i, ref in enumerate((first_ref, second_ref, crossed_ref)):

            @pl.when(kind == i)
            def _(ref=ref, k=k, tile=tile):
                returned_copy(ref, k, tile).start()

    product = squares = 0.0
    for k, tile in enumerate(tiles(features)):
        up_copy(k, tile).wait()
        returned_copy(first_ref, k, tile).wait()
        inputs = returned_ref[:, tile]
        product += dot(up_ref[:, tile], inputs, 1, 1)
        squares += squares_of(inputs)
    out_ref[:rank, :] = product.astype(out_ref.dtype)
    out_ref[rank:, :] = row_sums(squares).astype(out_ref.dtype)


def second_products(up_full, inputs):
    rank, features = up_full.shape
    rows = inputs[0].shape[0]
    return call(
        second_kernel, "second_products", (up_full, *inputs),
        [struct(rank + EXTRA, rows), struct(rows, features)],
        [pltpu.VMEM(up_full.shape, jnp.bfloat16), pltpu.SemaphoreType.DMA((2, features // TILE))],
        2 * rank * rows * features, (0, 1, 2, 3),
    )


def output_kernel(parts_ref, weights_ref, input_ref, cotangent_ref, out_ref, product_ref, up_ref):
    rank = product_ref.shape[0]
    scale = lax.rsqrt(parts_ref[rank : rank + 1, :] / D + epsilon)
    act = gated(parts_ref[:rank, :] * scale)[0].astype(jnp.bfloat16)
    product = 0.0
    for tile in tiles(input_ref.shape[1]):
        down = down_rows(weights_ref, tile)
        out = input_ref[:, tile].astype(jnp.float32) + dot(act, down, 0, 0)
        out_ref[:, tile] = out.astype(out_ref.dtype)
        product += dot(down, cotangent_ref[:, tile], 1, 1)
        up_ref[:, tile] = up_rows(weights_ref, tile)
    product_ref[...] = product


def forward_output(parts, weights, inputs, cotangent):
    group, own_rank, features = weights.shape
    rank, rows = group * own_rank // 2, inputs.shape[0]
    return call(
        output_kernel, "forward_output", (parts, weights, inputs, cotangent),
        [struct(*inputs.shape), struct(rank, rows, dtype=jnp.float32), struct(rank, features)],
        [], 4 * rank * rows * features,
    )


def input_kernel(parts_ref, grad_act_ref, up_ref, returned_ref, cotangent_ref, grad_ref, terms_ref):
    group, own_rank, _ = terms_ref.shape
    rank, rows = grad_act_ref.shape
    features = up_ref.shape[1]
    parts = jnp.sum(parts_ref[...].astype(jnp.float32), axis=0)
    back_proj = parts[:rank]
    scale = lax.rsqrt(parts[rank:] / D + epsilon)
    value, slope = gated(back_proj * scale[:1])
    grad_hidden = grad_act_ref[...] * slope
    proj = (grad_hidden * scale[:1]).astype(jnp.bfloat16)
    grad_scale = jnp.sum(grad_hidden * back_proj, axis=0, keepdims=True)
    pull = (-(scale * scale * scale) * grad_scale / D).T[:, :1]
    terms_ref[:, :, features:] = value.astype(terms_ref.dtype).reshape(group, own_rank, rows)
    for tile in tiles(features):
        returned = returned_ref[:, tile]
        grad = cotangent_ref[:, tile].astype(jnp.float32) + dot(proj, up_ref[:, tile], 0, 0)
        grad_ref[:, tile] = (grad + returned.astype(jnp.float32) * pull).astype(grad_ref.dtype)
        term = dot(proj, returned, 1, 0).astype(terms_ref.dtype)
        terms_ref[:, :, tile] = term.reshape(group, own_rank, TILE)


def input_gradient(parts, grad_act, up_full, returned, cotangent):
    rank, features = up_full.shape
    rows, group = returned.shape[0], lax.axis_size("dp")
    return call(
        input_kernel, "input_gradient", (parts, grad_act, up_full, returned, cotangent),
        [struct(rows, features), struct(group, rank // group, features + rows)], [], 4 * rank * rows * features,
    )


def weight_kernel(terms_ref, cotangents_ref, up_ref, down_ref):
    group, rows, features = cotangents_ref.shape
    acts = [terms_ref[k, :, features:] for k in range(group)]
    for tile in tiles(features):
        up_ref[:, tile] = jnp.sum(terms_ref[:, :, tile].astype(jnp.float32), axis=0).astype(up_ref.dtype)
        down = sum(dot(acts[k], cotangents_ref[k, :, tile], 1, 0) for k in range(group))
        down_ref[:, tile] = down.astype(down_ref.dtype)


def weight_gradients(terms, cotangents):
    group, rows, features = cotangents.shape
    share = (terms.shape[1], features)
    return call(
        weight_kernel, "weight_gradients", (terms, cotangents),
        [struct(*share)] * 2, [], 2 * group * rows * share[0] * features,
    )


def forward(weights, forward_in, cotangent):
    parts = summed(first_products(weights, forward_in), "mp")
    output, product, up_full = forward_output(parts, weights, forward_in, cotangent)
    return shifted(output, "pipe", 1), summed(product, "mp"), up_full


def beside(weights, copies, forward_in, cotangent):
    cotangents = lax.all_to_all(copies, "dp", split_axis=0, concat_axis=0, tiled=True)
    return *staged("mp", forward, weights, forward_in, cotangent), cotangents


def ahead(forward_in, cotangent, up_proj, down_proj, stash):
    group = lax.axis_size("dp")
    _, second, crossing = stash_routes(lax.axis_size("pipe"))
    copies = [jnp.broadcast_to(w[None], (group,) + w.shape) for w in (up_proj, down_proj)]
    weights = lax.all_to_all(jnp.concatenate(copies, 1), "dp", split_axis=0, concat_axis=0, tiled=True)
    crossed = lax.ppermute(stash, "pipe", [(i, i ^ 1) for i, _ in crossing])
    copies = jnp.broadcast_to(cotangent[None], (group,) + cotangent.shape)
    copies, crossed = lax.optimization_barrier((copies, crossed))
    returned_second = lax.ppermute(stash, "pipe", second)
    returned_crossed = lax.ppermute(crossed, "pipe", [(i ^ 1, target) for i, target in crossing])
    act_next, grad_act, up_full, cotangents = staged("mp", beside, weights, copies, forward_in, cotangent)
    return act_next, grad_act, up_full, cotangents, returned_second, returned_crossed


def backward(returned, cotangent, up_full, grad_act):
    parts, returned = second_products(up_full, returned)
    return input_gradient(spread(parts, "mp"), grad_act, up_full, returned, cotangent)


def hold_kernel(source_ref, out_ref):
    out_ref[...] = source_ref[...]


def held(block):
    return call(hold_kernel, "held", (block,), struct(*block.shape), [], 0)


def last_terms(terms, cotangents, act_next):
    terms = lax.all_to_all(terms, "dp", split_axis=0, concat_axis=0, tiled=True)
    return *weight_gradients(terms, cotangents), held(act_next)


def shards(act_in, grad_in, stash_far, up_proj, down_proj):
    cotangent = grad_in[0]
    first = stash_routes(lax.axis_size("pipe"))[0]
    returned = lax.ppermute(stash_far[0], "pipe", first)
    act_next, grad_act, up_full, cotangents, *returned_later = staged(
        "dp", ahead, act_in[0], cotangent, up_proj[0].T, down_proj[0], stash_far[0]
    )
    grad_input, terms = staged("dp", backward, [returned, *returned_later], cotangent, up_full, grad_act)
    grad_prev = shifted(grad_input, "pipe", -1)
    up_grad, down_grad, act_next = staged("dp", last_terms, terms, cotangents, act_next)
    return act_next[None], grad_prev[None], up_grad.T[None], down_grad[None]


def solution(mesh):
    in_specs = (
        P("pipe", "dp", "mp"),
        P("pipe", "dp", "mp"),
        P("pipe", "dp", "mp"),
        P("pipe", "mp", "dp"),
        P("pipe", "dp", "mp"),
    )
    out_specs = (
        P("pipe", "dp", "mp"),
        P("pipe", "dp", "mp"),
        P("pipe", "mp", "dp"),
        P("pipe", "dp", "mp"),
    )
    return jax.shard_map(shards, mesh=mesh, in_specs=in_specs, out_specs=out_specs, check_vma=False)
```
